512 devices in a mesh: scan: 128 (over z, y, core), mode: 4 (over x).
Axes of the slice: x: 4, y: 8, z: 8, core: 2. Of those that a mesh axis runs over, the one named last changes fastest.
Arguments:
- object_tiles: float32 [128, 2, 256, 256], P('scan'), may hold values from -6 to 6
- probe: float32 [4, 2, 256, 256], P('mode'), may hold values from -4 to 4
- measured: float32 [128, 256, 256], P('scan'), may hold values from 0.5 to 4
- cover: int32 [128], P('scan'), may hold values from 0 to 127, as said below
- counts: int32 [128], P('scan'), may hold values from 1 to 1, as said below
- phase: float32 [256, 256], replicated, may hold values from -3.140625 to 3.140625
Outputs:
- object_grad: float32 [128, 2, 256, 256], P('scan')
- probe_grad: float32 [4, 2, 256, 256], P('mode')
- loss: float32 [], replicated
The draws below stay inside these ranges and needn't reach their ends.
Inputs may be any that keep to these rules, and one draw needn't show every extreme that they name: The slots of group g cover tiles g - 2 to g + 2 only, within the object. `counts`: every group's single slot is live.
All inputs are finite; a program needn't handle non-finite values.
Results may differ from the reference program's by a relative error of at most 0.00019.
Values sent between devices are 32-bit elements; how exact they have to be, the bound alone decides.
No kernel may reach another device: no remote copies, remote signals or barrier semaphores. Data moves between devices by JAX's collectives and lax.ppermute only.
A program may use at most 64 MiB of HBM per device.

```python
import jax
import jax.numpy as jnp
from jax import lax

P_SIZE = 256
MODES = 4
POS_DEV = 1
REACH = 2
NT = 128
NPOS = 128


def draw_cover(key, part):
    key = jax.random.fold_in(key, 11)
    offsets = jax.random.randint(key, (NPOS,), -REACH, REACH + 1)
    groups = jnp.arange(NPOS, dtype=jnp.int32) // POS_DEV
    return jnp.clip(groups + offsets, 0, NT - 1).astype(jnp.int32)


def draw_counts(key, part):
    key = jax.random.fold_in(key, 23)
    key_one, key_two = jax.random.split(key)
    values = jax.random.randint(key_one, (NT,), 1, POS_DEV + 1)
    busiest = jax.random.randint(key_two, (), 0, NT)
    return jnp.where(jnp.arange(NT) == busiest, POS_DEV, values).astype(jnp.int32)


def levels(own_key, shape, cuts, least, largest):
    level = 1.0
    for position, parts in cuts:
        draws = jax.random.uniform(jax.random.fold_in(jax.random.fold_in(own_key, 6), position), (parts,), jnp.float32, least / len(cuts), largest / len(cuts))
        level = level * jnp.repeat(jnp.exp(draws), shape[position] // parts).reshape((-1,) + (1,) * (len(shape) - 1 - position))
    return level


def gaussian(stream_key, extent, width, limit, pieces=(), kind=jnp.bfloat16):
    loudness = levels(stream_key, extent, pieces, -0.22, 0.18) if pieces else 1.0
    drawn = jax.random.normal(stream_key, extent, jnp.float32) * width * loudness
    return jnp.minimum(jnp.maximum(drawn, -limit), limit).astype(kind)


def setup_inputs(seed: int = 0) -> dict:
    keys = jax.random.split(jax.random.key(seed), 7)
    return {
        "object_tiles": gaussian(keys[0], (NT, 2, P_SIZE, P_SIZE), 1.0, 6.0, ((0, 128),), jnp.float32),
        "probe": gaussian(keys[1], (MODES, 2, P_SIZE, P_SIZE), 0.5, 4.0, ((0, 4),), jnp.float32),
        "measured": jnp.clip(0.5 + 3.5 * jax.random.uniform(keys[2], (NPOS, P_SIZE, P_SIZE), jnp.float32) ** levels(keys[2], (NPOS, P_SIZE, P_SIZE), ((0, 128),), -0.2, 0.2), 0.5, 4.0),
        "cover": draw_cover(jax.random.fold_in(keys[6], 71), 0),
        "counts": draw_counts(jax.random.fold_in(keys[6], 71), 0),
        "phase": jnp.clip(jax.random.uniform(keys[5], (P_SIZE, P_SIZE), jnp.float32, -3.140625, 3.140625), -3.140625, 3.140625),
    }


def reference(object_tiles, probe, measured, cover, counts, phase):
    tiles_complex = object_tiles[:, 0] + 1j * object_tiles[:, 1]
    modes_complex = probe[:, 0] + 1j * probe[:, 1]
    kernel = jnp.cos(phase) + 1j * jnp.sin(phase)
    slot_index = jnp.arange(NPOS, dtype=jnp.int32)
    alive_mask = (slot_index % POS_DEV < counts[slot_index // POS_DEV]).astype(jnp.float32)

    def visit(carry, items):
        object_sum, probe_sum, loss_sum = carry
        tile_id, amplitude, alive = items
        patch = tiles_complex[tile_id]
        exit_wave = modes_complex * patch[None]
        wavefield = jnp.fft.ifft2(kernel * jnp.fft.fft2(exit_wave))
        intensity = lax.optimization_barrier(jnp.sum(jnp.real(wavefield) ** 2 + jnp.imag(wavefield) ** 2, axis=0))
        modulus = jnp.sqrt(intensity + 1.0)
        mismatch = modulus - amplitude
        weight = alive * mismatch / modulus
        back_field = jnp.fft.ifft2(jnp.conj(kernel) * jnp.fft.fft2(weight[None] * wavefield))
        object_sum = object_sum.at[tile_id].add(lax.optimization_barrier(jnp.sum(jnp.conj(modes_complex) * back_field, axis=0)))
        probe_sum = probe_sum + jnp.conj(patch)[None] * back_field
        loss_sum = loss_sum + alive * jnp.sum(mismatch * mismatch)
        return ((object_sum, probe_sum, loss_sum), None)
    start = (jnp.zeros_like(tiles_complex), jnp.zeros_like(modes_complex), jnp.zeros((), measured.dtype))
    (object_sum, probe_sum, loss_sum), unused = lax.scan(visit, start, (cover, measured, alive_mask))
    object_grad = jnp.stack([jnp.real(object_sum), jnp.imag(object_sum)], axis=1).astype(object_tiles.dtype)
    probe_grad = jnp.stack([jnp.real(probe_sum), jnp.imag(probe_sum)], axis=1).astype(probe.dtype)
    loss = loss_sum / (NPOS * P_SIZE * P_SIZE)
    return (object_grad, probe_grad, loss)
```

```python
import functools
import math

import jax
import jax.numpy as jnp
import ml_dtypes
import numpy as np
from jax import lax
from jax.experimental import pallas as pl
from jax.experimental.pallas import tpu as pltpu
from jax.sharding import Mesh
from jax.sharding import PartitionSpec as P

REACH = 2
SCAN = ("z", "y", "core")
PLANE = ("z", "y")
VMEM = pl.BlockSpec(memory_space=pltpu.VMEM)
SMEM = pl.BlockSpec(memory_space=pltpu.SMEM)
FLAG_ROWS = 8


def moved(block, axis, distance):
    size = lax.axis_size(axis)
    return lax.ppermute(block, axis, [(i, (i + distance) % size) for i in range(size)])


def split_tables(width):
    half = width // 2
    freq, place = np.arange(half)[:, None], np.arange(half)[None, :]
    out = []
    for parity in (0, 1):
        angle = ((2 * freq + parity) * place % width) * (2.0 * np.pi / width)
        cosine, sine = np.cos(angle), np.sin(angle)
        real_form = np.block([[cosine, sine], [-sine, cosine]])
        high = real_form.astype(np.float32).astype(ml_dtypes.bfloat16)
        low = (real_form - high.astype(np.float64)).astype(np.float32).astype(ml_dtypes.bfloat16)
        out += [high, low, np.ascontiguousarray(high.T), np.ascontiguousarray(low.T)]
    return np.stack(out)


def permutation(width):
    half = width // 2
    matrix = np.zeros((width, width), np.float32)
    for parity in (0, 1):
        for index in range(half):
            matrix[2 * index + parity, parity * half + index] = 1.0
    return np.stack([matrix, matrix.T]).astype(ml_dtypes.bfloat16)


def halves(value):
    high = value.astype(jnp.bfloat16)
    return high, (value - high.astype(jnp.float32)).astype(jnp.bfloat16)


def dot(left, right):
    return jnp.dot(left, right, preferred_element_type=jnp.float32)


def table_times(high, low, field):
    field_high, field_low = halves(field)
    return dot(
        jnp.concatenate([high, high, low], axis=1),
        jnp.concatenate([field_high, field_low, field_high], axis=0),
    )


def times_table(field, high, low):
    field_high, field_low = halves(field)
    return dot(
        jnp.concatenate([field_high, field_low, field_high], axis=1),
        jnp.concatenate([high, high, low], axis=0),
    )


def rows(*blocks):
    return jnp.concatenate(blocks, axis=0)


def cols(*blocks):
    return jnp.concatenate(blocks, axis=1)


def propagated(real, imag, tables, kernel):
    half = real.shape[0] // 2
    top, bottom = slice(0, half), slice(half, 2 * half)
    sums = rows(real[top] + real[bottom], imag[top] + imag[bottom])
    diffs = rows(real[top] - real[bottom], imag[top] - imag[bottom])
    bands = [
        table_times(tables[4 * p], tables[4 * p + 1], part) for p, part in ((0, sums), (1, diffs))
    ]
    left, right = slice(0, half), slice(half, 2 * half)
    plus = rows(*[cols(b[top, left] + b[top, right], b[bottom, left] + b[bottom, right]) for b in bands])
    minus = rows(*[cols(b[top, left] - b[top, right], b[bottom, left] - b[bottom, right]) for b in bands])
    back = []
    for q, part in ((0, plus), (1, minus)):
        freq = times_table(part, tables[4 * q + 2], tables[4 * q + 3])
        freq_real, freq_imag = freq[:, left], freq[:, right]
        kernel_real, kernel_imag = kernel(q)
        turned = cols(
            kernel_real * freq_real - kernel_imag * freq_imag,
            kernel_real * freq_imag + kernel_imag * freq_real,
        )
        back.append(times_table(turned, tables[4 * q], tables[4 * q + 1]))
    total, gap = back[0] + back[1], back[0] - back[1]
    out = []
    for p, band in ((0, top), (1, bottom)):
        stacked = rows(cols(total[band, left], gap[band, left]), cols(total[band, right], gap[band, right]))
        out.append(table_times(tables[4 * p + 2], tables[4 * p + 3], stacked))
    total, gap = out[0] + out[1], out[0] - out[1]
    return rows(total[top], gap[top]), rows(total[bottom], gap[bottom])


SIN_TERMS = [(-1.0) ** k / math.factorial(2 * k + 1) for k in range(7)]
COS_TERMS = [(-1.0) ** k / math.factorial(2 * k) for k in range(8)]


def horner(terms, square):
    total = jnp.full_like(square, terms[-1])
    for term in terms[-2::-1]:
        total = total * square + term
    return total


def cos_sin(phase):
    angle = phase * 0.5
    square = angle * angle
    sine = angle * horner(SIN_TERMS, square)
    cosine = horner(COS_TERMS, square)
    return 1.0 - 2.0 * sine * sine, 2.0 * sine * cosine


def forward_kernel(tile, probe, phase, tables, order, wave, power, turn):
    width = phase.shape[-1]
    half = width // 2
    scale = 1.0 / (width * width)
    rest = phase[...]
    ordered = None
    for _ in range(3):
        piece = rest.astype(jnp.bfloat16)
        rest = rest - piece.astype(jnp.float32)
        piece = dot(order[1], dot(piece, order[0]).astype(jnp.bfloat16))
        ordered = piece if ordered is None else ordered + piece
    cosine, sine = cos_sin(ordered)
    turn[0] = cosine * scale
    turn[1] = sine * scale
    exit_real = probe[0] * tile[0] - probe[1] * tile[1]
    exit_imag = probe[0] * tile[1] + probe[1] * tile[0]

    def kernel(q):
        lanes = slice(q * half, q * half + half)
        return turn[0, :, lanes], turn[1, :, lanes]

    real, imag = propagated(exit_real, exit_imag, [tables[i] for i in range(8)], kernel)
    wave[0] = real
    wave[1] = imag
    power[...] = real * real + imag * imag


def backward_kernel(
    place, tile, probe, wave, turn, tables, own, one, two, three, slot, *refs
):
    slots, (keep, send, tile_terms) = (slot,) + refs[: 2 * REACH], refs[2 * REACH :]
    width = own.shape[-1]
    half = width // 2
    home = place[0].astype(jnp.float32)
    core = place[1]
    intensity = (own[...] + one[...]) + (two[...] + three[...])
    modulus = jnp.sqrt(intensity + 1.0)
    mismatch_sum = jnp.zeros_like(modulus)
    squares = jnp.zeros_like(modulus)
    for ref in slots:
        chosen = (ref[width : width + 1, :] == home).astype(jnp.float32)
        mismatch = chosen * (modulus - ref[:width, :])
        mismatch_sum += mismatch
        squares += mismatch * mismatch
    weight = mismatch_sum / modulus

    def kernel(q):
        lanes = slice(q * half, q * half + half)
        return turn[0, :, lanes], -turn[1, :, lanes]

    real, imag = propagated(weight * wave[0], weight * wave[1], [tables[i] for i in range(8)], kernel)
    tile_terms[0] = probe[0] * real + probe[1] * imag
    tile_terms[1] = probe[0] * imag - probe[1] * real
    terms = (tile[0] * real + tile[1] * imag, tile[0] * imag - tile[1] * real)
    chunks = keep.shape[0] // 16 - 1
    first = core == 0
    for side in (0, 1):
        lanes = slice(side * half, side * half + half)
        for ref, value in (
            (keep, jnp.where(first, terms[0][:, lanes], terms[1][:, lanes])),
            (send, jnp.where(first, terms[1][:, lanes], terms[0][:, lanes])),
        ):
            ref[side * width : (side + 1) * width, :] = value
    loss = jnp.full((8, 128), jnp.sum(squares))
    keep[2 * width :, :] = loss
    send[2 * width :, :] = loss


def pair_kernel(keep, received, chunks):
    total = keep[...] + received[...]
    count = chunks.shape[0]
    chunks[:, 0:8, :] = total[: 8 * count].reshape(count, 8, 128)
    chunks[:, 8:16, :] = jnp.broadcast_to(total[8 * count :][None], (count, 8, 128))


def gather_kernel(arrived, spread, loss):
    total = jnp.sum(arrived[...], axis=0)
    spread[...] = jnp.broadcast_to(total[None, :8], spread.shape)
    loss[...] = total[8:]


def finish_kernel(place, mine, other, objects, probe_total, object_total):
    first = place[1] == 0
    width = probe_total.shape[-1]
    half = width // 2
    blocks = mine.shape[0] // 2
    for side in (0, 1):
        lanes = slice(side * half, side * half + half)
        here = mine[side * blocks : (side + 1) * blocks].reshape(width, half)
        there = other[side * blocks : (side + 1) * blocks].reshape(width, half)
        probe_total[0, 0, :, lanes] = jnp.where(first, here, there)
        probe_total[0, 1, :, lanes] = jnp.where(first, there, here)
    object_total[0] = (objects[0] + objects[1]) + (objects[2] + objects[3])


def struct(*shape):
    return jax.ShapeDtypeStruct(shape, jnp.float32)


def call(kernel, outs, name, scalars=0, operands=0):
    return pl.pallas_call(
        kernel,
        out_shape=outs,
        in_specs=[SMEM] * scalars + [VMEM] * operands,
        out_specs=jax.tree.map(lambda _: VMEM, outs),
        compiler_params=pltpu.CompilerParams(vmem_limit_bytes=24 * 1024 * 1024),
        name=name,
    )


def body(scan_size, object_tiles, probe, measured, cover, counts, phase):
    width = phase.shape[-1]
    tables = jnp.asarray(split_tables(width))
    order = jnp.asarray(permutation(width))
    home = lax.axis_index(SCAN)
    place = jnp.stack([home + 1, lax.axis_index("core")]).astype(jnp.int32)
    marker = jnp.where(counts[0] > 0, cover[0] + 1, 0).astype(jnp.float32)
    slot = jnp.concatenate([measured[0], jnp.broadcast_to(marker, (FLAG_ROWS, width))])
    around = [
        lax.ppermute(slot, SCAN, [(i, (i + d) % scan_size) for i in range(scan_size)])
        for d in range(-REACH, REACH + 1)
        if d
    ]
    wave, power, turn = call(
        forward_kernel,
        (struct(2, width, width), struct(width, width), struct(2, width, width)),
        "forward",
        operands=5,
    )(object_tiles[0], probe[0], phase, tables, order)
    powers = [moved(power, "mode", d) for d in (1, 2, 3)]
    keep, send, tile_terms = call(
        backward_kernel,
        (struct(2 * width + 8, 128), struct(2 * width + 8, 128), struct(2, width, width)),
        "backward",
        scalars=1,
        operands=10 + 2 * REACH,
    )(place, object_tiles[0], probe[0], wave, turn, tables, power, *powers, slot, *around)
    objects = lax.all_gather(tile_terms, "mode")
    received = moved(send, "core", 1)
    peers = lax.axis_size(PLANE)
    chunks = call(pair_kernel, struct(peers, 16, 128), "pair", operands=2)(keep, received)
    arrived = lax.all_to_all(chunks, PLANE, 0, 0, tiled=True)
    spread, loss = call(
        gather_kernel, (struct(peers, 8, 128), struct(8, 128)), "gather", operands=1
    )(arrived)
    mine = lax.all_to_all(spread, PLANE, 0, 0, tiled=True)
    other = moved(mine, "core", 1)
    probe_total, object_total = call(
        finish_kernel,
        (struct(1, 2, width, width), struct(1, 2, width, width)),
        "finish",
        scalars=1,
        operands=3,
    )(place, mine, other, objects)
    return object_total, probe_total, loss[0, 0] / (scan_size * width * width)


def solution(mesh):
    scan_size, modes = mesh.shape["scan"], mesh.shape["mode"]
    cube = Mesh(mesh.devices.reshape(8, 8, 2, modes), ("z", "y", "core", "mode"))
    return jax.shard_map(
        functools.partial(body, scan_size),
        mesh=cube,
        in_specs=(
            P(SCAN, None, None, None),
            P("mode", None, None, None),
            P(SCAN, None, None),
            P(SCAN),
            P(SCAN),
            P(),
        ),
        out_specs=(P(SCAN, None, None, None), P("mode", None, None, None), P()),
        check_vma=False,
    )
```

```python
import functools
import math

import jax
import jax.numpy as jnp
import ml_dtypes
import numpy as np
from jax import lax
from jax.experimental import pallas as pl
from jax.experimental.pallas import tpu as pltpu
from jax.sharding import Mesh
from jax.sharding import PartitionSpec as P

REACH = 2
SCAN = ("z", "y", "core")
PLANE = ("z", "y")
VMEM = pl.BlockSpec(memory_space=pltpu.VMEM)
FLAG_ROWS = 8
NO_TILE = -1000
CHUNK_ROWS = 17


def moved(block, axis, distance):
    size = lax.axis_size(axis)
    return lax.ppermute(block, axis, [(i, (i + distance) % size) for i in range(size)])


def split_tables(width):
    half = width // 2
    freq, place = np.arange(half)[:, None], np.arange(half)[None, :]
    out = []
    for parity in (0, 1):
        angle = ((2 * freq + parity) * place % width) * (2.0 * np.pi / width)
        cosine, sine = np.cos(angle), np.sin(angle)
        real_form = np.block([[cosine, sine], [-sine, cosine]])
        high = real_form.astype(np.float32).astype(ml_dtypes.bfloat16)
        low = (real_form - high.astype(np.float64)).astype(np.float32).astype(ml_dtypes.bfloat16)
        out += [high, low, np.ascontiguousarray(high.T), np.ascontiguousarray(low.T)]
    return np.stack(out)


def permutation(width):
    half = width // 2
    matrix = np.zeros((width, width), np.float32)
    for parity in (0, 1):
        for index in range(half):
            matrix[2 * index + parity, parity * half + index] = 1.0
    return np.stack([matrix, matrix.T]).astype(ml_dtypes.bfloat16)


def halves(value):
    high = value.astype(jnp.bfloat16)
    return high, (value - high.astype(jnp.float32)).astype(jnp.bfloat16)


def dot(left, right):
    return jnp.dot(left, right, preferred_element_type=jnp.float32)


def table_times(high, low, field):
    field_high, field_low = halves(field)
    return dot(
        jnp.concatenate([high, high, low], axis=1),
        jnp.concatenate([field_high, field_low, field_high], axis=0),
    )


def times_table(field, high, low):
    field_high, field_low = halves(field)
    return dot(
        jnp.concatenate([field_high, field_low, field_high], axis=1),
        jnp.concatenate([high, high, low], axis=0),
    )


def rows(*blocks):
    return jnp.concatenate(blocks, axis=0)


def cols(*blocks):
    return jnp.concatenate(blocks, axis=1)


def propagated(fields, tables, kernel):
    count, width = len(fields), fields[0][0].shape[0]
    half = width // 2
    top, bottom = slice(0, half), slice(half, 2 * half)
    left, right = top, bottom
    each = [slice(i * width, (i + 1) * width) for i in range(count)]
    sums = cols(*[rows(r[top] + r[bottom], i[top] + i[bottom]) for r, i in fields])
    diffs = cols(*[rows(r[top] - r[bottom], i[top] - i[bottom]) for r, i in fields])
    bands = [table_times(tables[4 * p], tables[4 * p + 1], part) for p, part in ((0, sums), (1, diffs))]
    plus, minus = [], []
    for one in each:
        for band in bands:
            b = band[:, one]
            plus.append(cols(b[top, left] + b[top, right], b[bottom, left] + b[bottom, right]))
            minus.append(cols(b[top, left] - b[top, right], b[bottom, left] - b[bottom, right]))
    back = []
    for q, part in ((0, rows(*plus)), (1, rows(*minus))):
        freq = times_table(part, tables[4 * q + 2], tables[4 * q + 3])
        kernel_real, kernel_imag = kernel(q)
        turned = []
        for one in each:
            freq_real, freq_imag = freq[one, left], freq[one, right]
            turned.append(
                cols(
                    kernel_real * freq_real - kernel_imag * freq_imag,
                    kernel_real * freq_imag + kernel_imag * freq_real,
                )
            )
        back.append(times_table(rows(*turned), tables[4 * q], tables[4 * q + 1]))
    total, gap = back[0] + back[1], back[0] - back[1]
    out = []
    for p in (0, 1):
        stacked = []
        for i in range(count):
            band = slice(i * width + p * half, i * width + (p + 1) * half)
            stacked.append(rows(cols(total[band, left], gap[band, left]), cols(total[band, right], gap[band, right])))
        out.append(table_times(tables[4 * p + 2], tables[4 * p + 3], cols(*stacked)))
    total, gap = out[0] + out[1], out[0] - out[1]
    return [
        (rows(total[top, one], gap[top, one]), rows(total[bottom, one], gap[bottom, one])) for one in each
    ]


SIN_TERMS = [(-1.0) ** k / math.factorial(2 * k + 1) for k in range(7)]
COS_TERMS = [(-1.0) ** k / math.factorial(2 * k) for k in range(8)]


def horner(terms, square):
    total = jnp.full_like(square, terms[-1])
    for term in terms[-2::-1]:
        total = total * square + term
    return total


def cos_sin(phase):
    angle = phase * 0.5
    square = angle * angle
    sine = angle * horner(SIN_TERMS, square)
    cosine = horner(COS_TERMS, square)
    return 1.0 - 2.0 * sine * sine, 2.0 * sine * cosine


def fetched(pairs, sems):
    copies = [pltpu.make_async_copy(src, dst, sems.at[i]) for i, (src, dst) in enumerate(pairs)]
    for copy in copies:
        copy.start()
    return copies


def waited(copies):
    for copy in copies:
        copy.wait()


def slot_kernel(cover, counts, measured, own, sems):
    width = own.shape[-1]
    copies = fetched([(measured.at[0], own.at[pl.ds(0, width)])], sems)
    marker = jnp.where(counts[...] > 0, cover[...], NO_TILE).astype(jnp.float32)
    own[width:, :] = jnp.broadcast_to(marker, (FLAG_ROWS, width))
    waited(copies)


def quarter(turn, sign):
    half = turn.shape[-1] // 2

    def kernel(q):
        lanes = slice(q * half, q * half + half)
        return turn[0, :, lanes], sign * turn[1, :, lanes]

    return kernel


def forward_kernel(
    phase_in, order_in, tile_in, probe_in, tables_in, wave_out, turn_out, power_out,
    phase, order, tile, probe, tables, wave, turn, power, sems,
):
    copies = fetched(
        [(phase_in, phase), (order_in, order), (tile_in, tile), (probe_in, probe), (tables_in, tables)], sems
    )
    width = phase.shape[-1]
    scale = 1.0 / (width * width)
    waited(copies[:2])
    rest = phase[...]
    ordered = None
    for _ in range(3):
        piece = rest.astype(jnp.bfloat16)
        rest = rest - piece.astype(jnp.float32)
        piece = dot(order[1], dot(piece, order[0]).astype(jnp.bfloat16))
        ordered = piece if ordered is None else ordered + piece
    cosine, sine = cos_sin(ordered)
    turn[0] = cosine * scale
    turn[1] = sine * scale
    outs = [pltpu.make_async_copy(turn, turn_out, sems.at[5])]
    outs[0].start()
    waited(copies[2:4])
    exit_real = probe[0] * tile[0] - probe[1] * tile[1]
    exit_imag = probe[0] * tile[1] + probe[1] * tile[0]
    waited(copies[4:])
    [(real, imag)] = propagated([(exit_real, exit_imag)], [tables[i] for i in range(8)], quarter(turn, 1.0))
    power[...] = real * real + imag * imag
    for mode in range(power_out.shape[0]):
        outs.append(pltpu.make_async_copy(power, power_out.at[mode], sems.at[6 + mode]))
        outs[-1].start()
    wave[0] = real
    wave[1] = imag
    outs.append(pltpu.make_async_copy(wave, wave_out, sems.at[6 + power_out.shape[0]]))
    outs[-1].start()
    waited(outs)


def match(marker, tile_number):
    return (marker == tile_number).astype(jnp.float32)


def outbound_kernel(own_in, other_in, ahead, behind, extra, own, other, sems):
    for copy in fetched([(own_in, own), (other_in, other)], sems):
        copy.wait()
    width = own.shape[-1]
    squares = jnp.zeros((width, width), jnp.float32)
    for distance, ref in ((REACH, ahead), (-REACH, behind)):
        target = (lax.axis_index(SCAN) + distance).astype(jnp.float32)
        has_own = match(own[width : width + 1, :], target)
        has_other = match(other[width : width + 1, :], target)
        number = has_own + has_other
        share = 1.0 / jnp.maximum(number, 1.0)
        ref[:width, :] = (has_own * own[:width, :] + has_other * other[:width, :]) * share
        ref[width:, :] = jnp.broadcast_to(number, (FLAG_ROWS, width))
        gap = own[:width, :] - other[:width, :]
        squares += (0.5 * has_own * has_other) * (gap * gap)
    extra[...] = jnp.sum(squares.reshape(width // 8, 8, width), axis=0)


def main_kernel(
    extra,
    powers_in, own_in, other_in, ahead_in, behind_in, turn_in, wave_in, tables_in, tile_in, probe_in,
    chunks, terms_0, terms_1, terms_2, terms_3,
    powers, own, other, ahead, behind, turn, wave, tables, tile, probe, terms, sems,
):
    copies = fetched(
        [
            (powers_in, powers),
            (own_in, own),
            (other_in, other),
            (ahead_in, ahead),
            (behind_in, behind),
            (wave_in, wave),
            (tables_in, tables),
            (turn_in, turn),
            (tile_in, tile),
            (probe_in, probe),
        ],
        sems,
    )
    width = powers.shape[-1]
    half = width // 2
    home = lax.axis_index(SCAN).astype(jnp.float32)
    waited(copies[:5])
    modulus = jnp.sqrt((powers[0] + powers[1]) + (powers[2] + powers[3]) + 1.0)
    mismatch_sum = jnp.zeros_like(modulus)
    squares = jnp.zeros_like(modulus)
    for ref, number in (
        (own, match(own[width : width + 1, :], home)),
        (other, match(other[width : width + 1, :], home)),
        (ahead, ahead[width : width + 1, :]),
        (behind, behind[width : width + 1, :]),
    ):
        mismatch = modulus - ref[:width, :]
        scaled = number * mismatch
        mismatch_sum += scaled
        squares += scaled * mismatch
    weight = mismatch_sum / modulus
    waited(copies[5:8])
    [(real, imag)] = propagated(
        [(weight * wave[0], weight * wave[1])], [tables[i] for i in range(8)], quarter(turn, -1.0)
    )
    waited(copies[8:])
    for plane, value in enumerate((probe[0] * real + probe[1] * imag, probe[0] * imag - probe[1] * real)):
        terms[2 * plane] = value[:half]
        terms[2 * plane + 1] = value[half:]
    mode = lax.axis_index("mode")
    outs = []
    for step, out in enumerate((terms_0, terms_1, terms_2, terms_3)):
        outs.append(pltpu.make_async_copy(terms.at[lax.rem(mode + step, 4)], out, sems.at[10 + step]))
        outs[-1].start()
    loss = jnp.full((1, half), jnp.sum(squares) + jnp.sum(extra[...]))
    blocks = width // 8
    for plane, value in enumerate((tile[0] * real + tile[1] * imag, tile[0] * imag - tile[1] * real)):
        for block in range(blocks):
            lines = value[8 * block : 8 * block + 8]
            start = CHUNK_ROWS * (plane * blocks + block)
            chunks[start : start + 8, :] = lines[:, :half]
            chunks[start + 8 : start + 16, :] = lines[:, half:]
            chunks[start + 16 : start + 17, :] = loss
    waited(outs)


def object_kernel(own, one, two, three, spread):
    total = (own[...] + one[...]) + (two[...] + three[...])
    for mode in range(spread.shape[0]):
        spread[mode] = total


def finish_kernel(pieces, out):
    half = pieces.shape[1]
    for piece in range(pieces.shape[0]):
        out[0, piece // 2, half * (piece % 2) : half * (piece % 2 + 1), :] = pieces[piece]


def plane_kernel(arrived, total):
    rows_in = arrived[...]
    count = rows_in.shape[0] // CHUNK_ROWS
    parts = [rows_in[CHUNK_ROWS * i : CHUNK_ROWS * (i + 1)] for i in range(count)]
    while len(parts) > 1:
        parts = [parts[i] + parts[i + 1] for i in range(0, len(parts), 2)]
    total[: CHUNK_ROWS] = parts[0]
    total[CHUNK_ROWS:] = jnp.zeros_like(total[CHUNK_ROWS:])


def spread_kernel(one, two, spread, loss):
    total = one[...] + two[...]
    lines = cols(total[0:8], total[8:16])
    spread[...] = jnp.broadcast_to(lines[None], spread.shape)
    loss[...] = jnp.broadcast_to(total[16:17], loss.shape)


def struct(*shape):
    return jax.ShapeDtypeStruct(shape, jnp.float32)


def call(kernel, name, operands, outs, microseconds, copied=(), far=(), direct=(), sems=0, scratch=()):
    specs, placed = [], []
    anywhere = pl.BlockSpec(memory_space=pl.ANY)
    for index, operand in enumerate(operands):
        specs.append(anywhere if index in copied or index in far else VMEM)
        placed.append(pltpu.with_memory_space_constraint(operand, pltpu.HBM) if index in far else operand)
    scratch_shapes = [pltpu.VMEM(operands[i].shape, operands[i].dtype) for i in copied]
    for entry in scratch:
        buffer = outs[entry] if isinstance(entry, int) else entry
        scratch_shapes.append(pltpu.VMEM(buffer.shape, buffer.dtype))
    count = len(copied) + len(direct) + sems
    if count:
        scratch_shapes.append(pltpu.SemaphoreType.DMA((count,)))
    return pl.pallas_call(
        kernel,
        out_shape=[pltpu.HBM(o.shape, o.dtype) if i in direct else o for i, o in enumerate(outs)],
        in_specs=specs,
        out_specs=[anywhere if i in direct else VMEM for i in range(len(outs))],
        scratch_shapes=scratch_shapes,
        cost_estimate=pl.CostEstimate(
            flops=int(microseconds * 1.1e9), bytes_accessed=1 << 20, transcendentals=0
        ),
        compiler_params=pltpu.CompilerParams(vmem_limit_bytes=32 * 1024 * 1024),
        name=name,
    )(*placed)


def body(scan_size, object_tiles, probe, measured, cover, counts, phase):
    width = phase.shape[-1]
    modes = lax.axis_size("mode")
    peers = lax.axis_size(PLANE)
    tables = jnp.asarray(split_tables(width))
    order = jnp.asarray(permutation(width))
    tile, own_probe = object_tiles[0], probe[0]
    square, plane_pair = struct(width, width), struct(2, width, width)
    slot = struct(width + FLAG_ROWS, width)
    wave, turn, power = call(
        forward_kernel, "forward", (phase, order, tile, own_probe, tables),
        [plane_pair, plane_pair, struct(modes, width, width)], 4,
        copied=(0, 1, 2, 3, 4), far=(0, 1, 2, 3, 4), direct=(0, 1, 2), sems=modes - 1, scratch=(0, 1, square),
    )
    powers = lax.all_to_all(power, "mode", 0, 0, tiled=True)
    [own] = call(slot_kernel, "slot", (cover.reshape(1, 1), counts.reshape(1, 1), measured), [slot], 1, far=(2,), sems=1)
    other = moved(own, "core", 1)
    ahead, behind, extra = call(
        outbound_kernel, "outbound", (own, other), [slot, slot, struct(8, width)], 1, copied=(0, 1)
    )
    from_behind = lax.ppermute(ahead, SCAN, [(i, (i + REACH) % scan_size) for i in range(scan_size)])
    from_ahead = lax.ppermute(behind, SCAN, [(i, (i - REACH) % scan_size) for i in range(scan_size)])
    quarter_plane = struct(width // 2, width)
    chunks, *terms = call(
        main_kernel, "main",
        (extra, powers, own, other, from_behind, from_ahead, turn, wave, tables, tile, own_probe),
        [struct(peers * CHUNK_ROWS, 128)] + [quarter_plane] * modes, 4,
        copied=tuple(range(1, 11)), far=(6, 7, 8, 9, 10), direct=tuple(range(1, 1 + modes)),
        scratch=(struct(modes, width // 2, width),),
    )
    arrived = lax.all_to_all(chunks.reshape(peers, 1, CHUNK_ROWS * 128), PLANE, 0, 0, tiled=True)
    pieces = [moved(terms[step], "mode", step) for step in range(1, modes)]
    arrived, *pieces = lax.optimization_barrier((arrived, *pieces))
    [part] = call(plane_kernel, "plane", (arrived.reshape(peers * CHUNK_ROWS, 128),), [struct(24, 128)], 1)
    [object_spread] = call(
        object_kernel, "object", (terms[0], *pieces), [struct(modes, width // 2, width)], 1
    )
    spread, loss = call(
        spread_kernel, "spread", (part, moved(part, "core", 1)), [struct(peers, 8, width), struct(8, 128)], 1
    )
    probe_total = lax.all_to_all(spread, PLANE, 0, 0, tiled=True)
    [object_total] = call(
        finish_kernel, "finish", (lax.all_to_all(object_spread, "mode", 0, 0, tiled=True),),
        [struct(1, 2, width, width)], 1,
    )
    return (
        object_total,
        probe_total.reshape(1, 2, width, width),
        loss[0, 0] / (scan_size * width * width),
    )


def solution(mesh):
    scan_size, modes = mesh.shape["scan"], mesh.shape["mode"]
    cube = Mesh(mesh.devices.reshape(8, 8, 2, modes), ("z", "y", "core", "mode"))
    return jax.shard_map(
        functools.partial(body, scan_size),
        mesh=cube,
        in_specs=(
            P(SCAN, None, None, None),
            P("mode", None, None, None),
            P(SCAN, None, None),
            P(SCAN),
            P(SCAN),
            P(),
        ),
        out_specs=(P(SCAN, None, None, None), P("mode", None, None, None), P()),
        check_vma=False,
    )
```

```python
import functools
import math

import jax
import jax.numpy as jnp
import ml_dtypes
import numpy as np
from jax import lax
from jax.experimental import pallas as pl
from jax.experimental.pallas import tpu as pltpu
from jax.sharding import Mesh
from jax.sharding import PartitionSpec as P

REACH = 2
SCAN = ("z", "y", "core")
PLANE = ("z", "y")
VMEM = pl.BlockSpec(memory_space=pltpu.VMEM)
SMEM = pl.BlockSpec(memory_space=pltpu.SMEM)
FLAG_ROWS = 8
NO_TILE = -1000
CHUNK_ROWS = 17


def moved(block, axis, distance):
    size = lax.axis_size(axis)
    return lax.ppermute(block, axis, [(i, (i + distance) % size) for i in range(size)])


def split_tables(width):
    half = width // 2
    freq, place = np.arange(half)[:, None], np.arange(half)[None, :]
    out = []
    for parity in (0, 1):
        angle = ((2 * freq + parity) * place % width) * (2.0 * np.pi / width)
        cosine, sine = np.cos(angle), np.sin(angle)
        real_form = np.block([[cosine, sine], [-sine, cosine]])
        high = real_form.astype(np.float32).astype(ml_dtypes.bfloat16)
        low = (real_form - high.astype(np.float64)).astype(np.float32).astype(ml_dtypes.bfloat16)
        out += [high, low, np.ascontiguousarray(high.T), np.ascontiguousarray(low.T)]
    return np.stack(out)


def permutation(width):
    half = width // 2
    matrix = np.zeros((width, width), np.float32)
    for parity in (0, 1):
        for index in range(half):
            matrix[2 * index + parity, parity * half + index] = 1.0
    return np.stack([matrix, matrix.T]).astype(ml_dtypes.bfloat16)


def halves(value):
    high = value.astype(jnp.bfloat16)
    return high, (value - high.astype(jnp.float32)).astype(jnp.bfloat16)


def dot(left, right):
    return jnp.dot(left, right, preferred_element_type=jnp.float32)


def table_times(high, low, field):
    field_high, field_low = halves(field)
    return dot(
        jnp.concatenate([high, high, low], axis=1),
        jnp.concatenate([field_high, field_low, field_high], axis=0),
    )


def times_table(field, high, low):
    field_high, field_low = halves(field)
    return dot(
        jnp.concatenate([field_high, field_low, field_high], axis=1),
        jnp.concatenate([high, high, low], axis=0),
    )


def rows(*blocks):
    return jnp.concatenate(blocks, axis=0)


def cols(*blocks):
    return jnp.concatenate(blocks, axis=1)


def propagated(fields, tables, kernel):
    count, width = len(fields), fields[0][0].shape[0]
    half = width // 2
    top, bottom = slice(0, half), slice(half, 2 * half)
    left, right = top, bottom
    each = [slice(i * width, (i + 1) * width) for i in range(count)]
    sums = cols(*[rows(r[top] + r[bottom], i[top] + i[bottom]) for r, i in fields])
    diffs = cols(*[rows(r[top] - r[bottom], i[top] - i[bottom]) for r, i in fields])
    bands = [table_times(tables[4 * p], tables[4 * p + 1], part) for p, part in ((0, sums), (1, diffs))]
    plus, minus = [], []
    for one in each:
        for band in bands:
            b = band[:, one]
            plus.append(cols(b[top, left] + b[top, right], b[bottom, left] + b[bottom, right]))
            minus.append(cols(b[top, left] - b[top, right], b[bottom, left] - b[bottom, right]))
    back = []
    for q, part in ((0, rows(*plus)), (1, rows(*minus))):
        freq = times_table(part, tables[4 * q + 2], tables[4 * q + 3])
        kernel_real, kernel_imag = kernel(q)
        turned = []
        for one in each:
            freq_real, freq_imag = freq[one, left], freq[one, right]
            turned.append(
                cols(
                    kernel_real * freq_real - kernel_imag * freq_imag,
                    kernel_real * freq_imag + kernel_imag * freq_real,
                )
            )
        back.append(times_table(rows(*turned), tables[4 * q], tables[4 * q + 1]))
    total, gap = back[0] + back[1], back[0] - back[1]
    out = []
    for p in (0, 1):
        stacked = []
        for i in range(count):
            band = slice(i * width + p * half, i * width + (p + 1) * half)
            stacked.append(rows(cols(total[band, left], gap[band, left]), cols(total[band, right], gap[band, right])))
        out.append(table_times(tables[4 * p + 2], tables[4 * p + 3], cols(*stacked)))
    total, gap = out[0] + out[1], out[0] - out[1]
    return [
        (rows(total[top, one], gap[top, one]), rows(total[bottom, one], gap[bottom, one])) for one in each
    ]


SIN_TERMS = [(-1.0) ** k / math.factorial(2 * k + 1) for k in range(7)]
COS_TERMS = [(-1.0) ** k / math.factorial(2 * k) for k in range(8)]


def horner(terms, square):
    total = jnp.full_like(square, terms[-1])
    for term in terms[-2::-1]:
        total = total * square + term
    return total


def cos_sin(phase):
    angle = phase * 0.5
    square = angle * angle
    sine = angle * horner(SIN_TERMS, square)
    cosine = horner(COS_TERMS, square)
    return 1.0 - 2.0 * sine * sine, 2.0 * sine * cosine


def fetched(pairs, sems):
    copies = [pltpu.make_async_copy(src, dst, sems.at[i]) for i, (src, dst) in enumerate(pairs)]
    for copy in copies:
        copy.start()
    return copies


def waited(copies):
    for copy in copies:
        copy.wait()


def quarter(turn, sign):
    half = turn.shape[-1] // 2

    def kernel(q):
        lanes = slice(q * half, q * half + half)
        return turn[0, :, lanes], sign * turn[1, :, lanes]

    return kernel


def forward_kernel(
    phase_in, order_in, tile_in, probe_in, tables_in, cover, counts, measured,
    own, wave_out, turn_out, power_out,
    phase, order, tile, probe, tables, wave, turn, power, sems,
):
    copies = fetched(
        [
            (phase_in, phase),
            (order_in, order),
            (tile_in, tile),
            (probe_in, probe),
            (tables_in, tables),
            (measured.at[0], own.at[pl.ds(0, own.shape[1])]),
        ],
        sems,
    )
    width = phase.shape[-1]
    scale = 1.0 / (width * width)
    waited(copies[:2])
    rest = phase[...]
    ordered = None
    for _ in range(3):
        piece = rest.astype(jnp.bfloat16)
        rest = rest - piece.astype(jnp.float32)
        piece = dot(order[1], dot(piece, order[0]).astype(jnp.bfloat16))
        ordered = piece if ordered is None else ordered + piece
    cosine, sine = cos_sin(ordered)
    turn[0] = cosine * scale
    turn[1] = sine * scale
    outs = [pltpu.make_async_copy(turn, turn_out, sems.at[6])]
    outs[0].start()
    waited(copies[2:4])
    exit_real = probe[0] * tile[0] - probe[1] * tile[1]
    exit_imag = probe[0] * tile[1] + probe[1] * tile[0]
    waited(copies[4:5])
    [(real, imag)] = propagated([(exit_real, exit_imag)], [tables[i] for i in range(8)], quarter(turn, 1.0))
    power[...] = real * real + imag * imag
    for mode in range(power_out.shape[0]):
        outs.append(pltpu.make_async_copy(power, power_out.at[mode], sems.at[7 + mode]))
        outs[-1].start()
    wave[0] = real
    wave[1] = imag
    outs.append(pltpu.make_async_copy(wave, wave_out, sems.at[7 + power_out.shape[0]]))
    outs[-1].start()
    waited(copies[5:])
    marker = jnp.where(counts[0] > 0, cover[0], NO_TILE).astype(jnp.float32)
    own[width:, :] = jnp.full((FLAG_ROWS, width), marker)
    waited(outs)


def match(marker, tile_number):
    return (marker == tile_number).astype(jnp.float32)


def outbound_kernel(own_in, other_in, ahead, behind, extra, own, other, sems):
    for copy in fetched([(own_in, own), (other_in, other)], sems):
        copy.wait()
    width = own.shape[-1]
    squares = jnp.zeros((width, width), jnp.float32)
    for distance, ref in ((REACH, ahead), (-REACH, behind)):
        target = (lax.axis_index(SCAN) + distance).astype(jnp.float32)
        has_own = match(own[width : width + 1, :], target)
        has_other = match(other[width : width + 1, :], target)
        number = has_own + has_other
        share = 1.0 / jnp.maximum(number, 1.0)
        ref[:width, :] = (has_own * own[:width, :] + has_other * other[:width, :]) * share
        ref[width:, :] = jnp.broadcast_to(number, (FLAG_ROWS, width))
        gap = own[:width, :] - other[:width, :]
        squares += (0.5 * has_own * has_other) * (gap * gap)
    extra[...] = jnp.sum(squares.reshape(width // 8, 8, width), axis=0)


def main_kernel(
    extra,
    powers_in, own_in, other_in, ahead_in, behind_in, turn_in, wave_in, tables_in, tile_in, probe_in,
    chunks_out, terms_out,
    powers, own, other, ahead, behind, turn, wave, tables, tile, probe, chunks, terms, sems,
):
    copies = fetched(
        [
            (powers_in, powers),
            (own_in, own),
            (other_in, other),
            (ahead_in, ahead),
            (behind_in, behind),
            (wave_in, wave),
            (tables_in, tables),
            (turn_in, turn),
            (tile_in, tile),
            (probe_in, probe),
        ],
        sems,
    )
    width = powers.shape[-1]
    half = width // 2
    home = lax.axis_index(SCAN).astype(jnp.float32)
    waited(copies[:5])
    modulus = jnp.sqrt((powers[0] + powers[1]) + (powers[2] + powers[3]) + 1.0)
    mismatch_sum = jnp.zeros_like(modulus)
    squares = jnp.zeros_like(modulus)
    for ref, number in (
        (own, match(own[width : width + 1, :], home)),
        (other, match(other[width : width + 1, :], home)),
        (ahead, ahead[width : width + 1, :]),
        (behind, behind[width : width + 1, :]),
    ):
        mismatch = modulus - ref[:width, :]
        scaled = number * mismatch
        mismatch_sum += scaled
        squares += scaled * mismatch
    weight = mismatch_sum / modulus
    waited(copies[5:8])
    [(real, imag)] = propagated(
        [(weight * wave[0], weight * wave[1])], [tables[i] for i in range(8)], quarter(turn, -1.0)
    )
    waited(copies[8:9])
    loss = jnp.full((1, half), jnp.sum(squares) + jnp.sum(extra[...]))
    blocks = width // 8
    outs = []
    for plane, value in enumerate((tile[0] * real + tile[1] * imag, tile[0] * imag - tile[1] * real)):
        for block in range(blocks):
            lines = value[8 * block : 8 * block + 8]
            start = CHUNK_ROWS * (plane * blocks + block)
            chunks[start : start + 8, :] = lines[:, :half]
            chunks[start + 8 : start + 16, :] = lines[:, half:]
            chunks[start + 16 : start + 17, :] = loss
        part = pl.ds(CHUNK_ROWS * blocks * plane, CHUNK_ROWS * blocks)
        outs.append(pltpu.make_async_copy(chunks.at[part], chunks_out.at[part], sems.at[10 + plane]))
        outs[-1].start()
    waited(copies[9:])
    terms[0] = probe[0] * real + probe[1] * imag
    terms[1] = probe[0] * imag - probe[1] * real
    outs.append(pltpu.make_async_copy(terms, terms_out, sems.at[12]))
    outs[-1].start()
    waited(outs)


def object_kernel(own_in, one_in, two_in, three_in, out, own, one, two, three, sems):
    waited(fetched([(own_in, own), (one_in, one), (two_in, two), (three_in, three)], sems))
    out[0] = (own[...] + one[...]) + (two[...] + three[...])


def plane_kernel(arrived, total):
    rows_in = arrived[...]
    count = rows_in.shape[0] // CHUNK_ROWS
    parts = [rows_in[CHUNK_ROWS * i : CHUNK_ROWS * (i + 1)] for i in range(count)]
    while len(parts) > 1:
        parts = [parts[i] + parts[i + 1] for i in range(0, len(parts), 2)]
    total[: CHUNK_ROWS] = parts[0]
    total[CHUNK_ROWS:] = jnp.zeros_like(total[CHUNK_ROWS:])


def spread_kernel(one, two, spread, loss):
    total = one[...] + two[...]
    lines = cols(total[0:8], total[8:16])
    spread[...] = jnp.broadcast_to(lines[None], spread.shape)
    loss[...] = jnp.broadcast_to(total[16:17], loss.shape)


def struct(*shape):
    return jax.ShapeDtypeStruct(shape, jnp.float32)


def call(kernel, name, operands, outs, microseconds, copied=(), far=(), direct=(), sems=0, scratch=()):
    specs, placed = [], []
    anywhere = pl.BlockSpec(memory_space=pl.ANY)
    for index, operand in enumerate(operands):
        if operand.dtype == jnp.int32:
            specs.append(SMEM)
        else:
            specs.append(anywhere if index in copied or index in far else VMEM)
        placed.append(pltpu.with_memory_space_constraint(operand, pltpu.HBM) if index in far else operand)
    scratch_shapes = [pltpu.VMEM(operands[i].shape, operands[i].dtype) for i in copied]
    for entry in scratch:
        buffer = outs[entry] if isinstance(entry, int) else entry
        scratch_shapes.append(pltpu.VMEM(buffer.shape, buffer.dtype))
    count = len(copied) + len(direct) + sems
    if count:
        scratch_shapes.append(pltpu.SemaphoreType.DMA((count,)))
    return pl.pallas_call(
        kernel,
        out_shape=[pltpu.HBM(o.shape, o.dtype) if i in direct else o for i, o in enumerate(outs)],
        in_specs=specs,
        out_specs=[anywhere if i in direct else VMEM for i in range(len(outs))],
        scratch_shapes=scratch_shapes,
        cost_estimate=pl.CostEstimate(
            flops=int(microseconds * 1.1e9), bytes_accessed=0, transcendentals=0
        ),
        compiler_params=pltpu.CompilerParams(vmem_limit_bytes=32 * 1024 * 1024),
        name=name,
    )(*placed)


def body(scan_size, object_tiles, probe, measured, cover, counts, phase):
    width = phase.shape[-1]
    modes = lax.axis_size("mode")
    peers = lax.axis_size(PLANE)
    tables = jnp.asarray(split_tables(width))
    order = jnp.asarray(permutation(width))
    tile, own_probe = object_tiles[0], probe[0]
    square, plane_pair = struct(width, width), struct(2, width, width)
    slot = struct(width + FLAG_ROWS, width)
    own, wave, turn, power = call(
        forward_kernel, "forward", (phase, order, tile, own_probe, tables, cover, counts, measured),
        [slot, plane_pair, plane_pair, struct(modes, width, width)], 4,
        copied=(0, 1, 2, 3, 4), far=(0, 1, 2, 3, 4, 7), direct=(1, 2, 3), sems=modes,
        scratch=(1, 2, square),
    )
    powers = lax.all_to_all(power, "mode", 0, 0, tiled=True)
    other = moved(own, "core", 1)
    ahead, behind, extra = call(
        outbound_kernel, "outbound", (own, other), [slot, slot, struct(8, width)], 1, copied=(0, 1)
    )
    from_behind = lax.ppermute(ahead, SCAN, [(i, (i + REACH) % scan_size) for i in range(scan_size)])
    from_ahead = lax.ppermute(behind, SCAN, [(i, (i - REACH) % scan_size) for i in range(scan_size)])
    chunks, terms = call(
        main_kernel, "main",
        (extra, powers, own, other, from_behind, from_ahead, turn, wave, tables, tile, own_probe),
        [struct(peers * CHUNK_ROWS, 128), plane_pair], 4,
        copied=tuple(range(1, 11)), far=(6, 7, 8, 9, 10), direct=(0, 1), sems=1, scratch=(0, 1),
    )
    arrived = lax.all_to_all(chunks.reshape(peers, 1, CHUNK_ROWS * 128), PLANE, 0, 0, tiled=True)
    others = [moved(terms, "mode", step) for step in (2, 1, 3)]
    [part] = call(plane_kernel, "plane", (arrived.reshape(peers * CHUNK_ROWS, 128),), [struct(24, 128)], 0)
    part_other = moved(part, "core", 1)
    spread, loss = call(
        spread_kernel, "spread", (part, part_other), [struct(peers, 8, width), struct(8, 128)], 0
    )
    probe_total = lax.all_to_all(spread, PLANE, 0, 0, tiled=True)
    [object_total] = call(
        object_kernel, "object", (terms, *others), [struct(1, 2, width, width)], 100, copied=(0, 1, 2, 3)
    )
    return (
        object_total,
        probe_total.reshape(1, 2, width, width),
        loss[0, 0] / (scan_size * width * width),
    )


def solution(mesh):
    scan_size, modes = mesh.shape["scan"], mesh.shape["mode"]
    cube = Mesh(mesh.devices.reshape(8, 8, 2, modes), ("z", "y", "core", "mode"))
    return jax.shard_map(
        functools.partial(body, scan_size),
        mesh=cube,
        in_specs=(
            P(SCAN, None, None, None),
            P("mode", None, None, None),
            P(SCAN, None, None),
            P(SCAN),
            P(SCAN),
            P(),
        ),
        out_specs=(P(SCAN, None, None, None), P("mode", None, None, None), P()),
        check_vma=False,
    )
```

```python
import functools
import math

import jax
import jax.numpy as jnp
import ml_dtypes
import numpy as np
from jax import lax
from jax.experimental import pallas as pl
from jax.experimental.pallas import tpu as pltpu
from jax.sharding import Mesh
from jax.sharding import PartitionSpec as P

SCAN = ("z", "y", "core")
PLANE = ("z", "y")
VMEM = pl.BlockSpec(memory_space=pltpu.VMEM)
SMEM = pl.BlockSpec(memory_space=pltpu.SMEM)
FLAG_ROWS = 8
NO_TILE = -1000
CHUNK_ROWS = 17


def moved(block, axis, distance):
    size = lax.axis_size(axis)
    return lax.ppermute(block, axis, [(i, (i + distance) % size) for i in range(size)])


def split_tables(width):
    half = width // 2
    freq, place = np.arange(half)[:, None], np.arange(half)[None, :]
    out = []
    for parity in (0, 1):
        angle = ((2 * freq + parity) * place % width) * (2.0 * np.pi / width)
        cosine, sine = np.cos(angle), np.sin(angle)
        real_form = np.block([[cosine, sine], [-sine, cosine]])
        high = real_form.astype(np.float32).astype(ml_dtypes.bfloat16)
        low = (real_form - high.astype(np.float64)).astype(np.float32).astype(ml_dtypes.bfloat16)
        out += [high, low]
    return np.stack(out + [np.ascontiguousarray(table.T) for table in out])


def permutation(width):
    half = width // 2
    matrix = np.zeros((width, width), np.float32)
    for parity in (0, 1):
        for index in range(half):
            matrix[2 * index + parity, parity * half + index] = 1.0
    return matrix.astype(ml_dtypes.bfloat16)


def halves(value):
    high = value.astype(jnp.bfloat16)
    return high, (value - high.astype(jnp.float32)).astype(jnp.bfloat16)


def dot(left, right):
    return jnp.dot(left, right, preferred_element_type=jnp.float32)


def table_times(high, low, field):
    field_high, field_low = halves(field)
    return dot(
        jnp.concatenate([high, high, low], axis=1),
        jnp.concatenate([field_high, field_low, field_high], axis=0),
    )


def times_table(field, high, low):
    field_high, field_low = halves(field)
    return dot(
        jnp.concatenate([field_high, field_low, field_high], axis=1),
        jnp.concatenate([high, high, low], axis=0),
    )


def rows(*blocks):
    return jnp.concatenate(blocks, axis=0)


def cols(*blocks):
    return jnp.concatenate(blocks, axis=1)


def waited(copies):
    for copy in copies:
        copy.wait()


def propagated(fields, tables, kernel, second=(), third=()):
    count, width = len(fields), fields[0][0].shape[0]
    half = width // 2
    top, bottom = slice(0, half), slice(half, 2 * half)
    left, right = top, bottom
    each = [slice(i * width, (i + 1) * width) for i in range(count)]
    sums = cols(*[rows(r[top] + r[bottom], i[top] + i[bottom]) for r, i in fields])
    diffs = cols(*[rows(r[top] - r[bottom], i[top] - i[bottom]) for r, i in fields])
    bands = [table_times(tables[2 * p], tables[2 * p + 1], part) for p, part in ((0, sums), (1, diffs))]
    plus, minus = [], []
    for one in each:
        for band in bands:
            b = band[:, one]
            plus.append(cols(b[top, left] + b[top, right], b[bottom, left] + b[bottom, right]))
            minus.append(cols(b[top, left] - b[top, right], b[bottom, left] - b[bottom, right]))
    back = []
    waited(second)
    freqs = [
        times_table(rows(*part), tables[2 * q + 4], tables[2 * q + 5]) for q, part in ((0, plus), (1, minus))
    ]
    waited(third)
    for q, freq in enumerate(freqs):
        kernel_real, kernel_imag = kernel(q)
        turned = []
        for one in each:
            freq_real, freq_imag = freq[one, left], freq[one, right]
            turned.append(
                cols(
                    kernel_real * freq_real - kernel_imag * freq_imag,
                    kernel_real * freq_imag + kernel_imag * freq_real,
                )
            )
        back.append(times_table(rows(*turned), tables[2 * q], tables[2 * q + 1]))
    total, gap = back[0] + back[1], back[0] - back[1]
    out = []
    for p in (0, 1):
        stacked = []
        for i in range(count):
            band = slice(i * width + p * half, i * width + (p + 1) * half)
            stacked.append(rows(cols(total[band, left], gap[band, left]), cols(total[band, right], gap[band, right])))
        out.append(table_times(tables[2 * p + 4], tables[2 * p + 5], cols(*stacked)))
    total, gap = out[0] + out[1], out[0] - out[1]
    return [
        (rows(total[top, one], gap[top, one]), rows(total[bottom, one], gap[bottom, one])) for one in each
    ]


SIN_TERMS = [(-1.0) ** k / math.factorial(2 * k + 1) for k in range(7)]
COS_TERMS = [(-1.0) ** k / math.factorial(2 * k) for k in range(8)]


def horner(terms, square):
    total = jnp.full_like(square, terms[-1])
    for term in terms[-2::-1]:
        total = total * square + term
    return total


def cos_sin(phase):
    angle = phase * 0.5
    square = angle * angle
    sine = angle * horner(SIN_TERMS, square)
    cosine = horner(COS_TERMS, square)
    return 1.0 - 2.0 * sine * sine, 2.0 * sine * cosine


def fetched(pairs, sems):
    copies = [pltpu.make_async_copy(src, dst, sems.at[i]) for i, (src, dst) in enumerate(pairs)]
    for copy in copies:
        copy.start()
    return copies


def quarter(turn, sign):
    half = turn.shape[-1] // 2

    def kernel(q):
        lanes = slice(q * half, q * half + half)
        return turn[0, :, lanes], sign * turn[1, :, lanes]

    return kernel


def forward_kernel(
    phase_in, order_in, tile_in, probe_in, tables_in, cover, counts, measured,
    own, wave_out, turn_out, power_out,
    order, tile, probe, tables, phase, wave, turn, power, sems,
):
    width = phase_in.shape[-1]
    half = width // 2
    copies = fetched(
        [
            (phase_in.at[:, pl.ds(0, half)], phase.at[0]),
            (phase_in.at[:, pl.ds(half, half)], phase.at[1]),
            (order_in, order),
            (tile_in, tile),
            (probe_in, probe),
            (tables_in.at[pl.ds(0, 4)], tables.at[pl.ds(0, 4)]),
            (tables_in.at[pl.ds(4, 4)], tables.at[pl.ds(4, 4)]),
            (measured.at[0], own.at[pl.ds(0, own.shape[1])]),
        ],
        sems,
    )
    scale = 1.0 / (width * width)
    waited(copies[:3])
    swap = order[...]
    rest = rows(*[cols(*[phase[h, pl.ds(p, half, stride=2), :] for h in (0, 1)]) for p in (0, 1)])
    ordered = None
    for _ in range(3):
        piece = rest.astype(jnp.bfloat16)
        rest = rest - piece.astype(jnp.float32)
        piece = dot(piece, swap)
        ordered = piece if ordered is None else ordered + piece
    cosine, sine = cos_sin(ordered)
    turn[0] = cosine * scale
    turn[1] = sine * scale
    outs = [pltpu.make_async_copy(turn, turn_out, sems.at[8])]
    outs[0].start()
    waited(copies[3:5])
    exit_real = probe[0] * tile[0] - probe[1] * tile[1]
    exit_imag = probe[0] * tile[1] + probe[1] * tile[0]
    waited(copies[5:6])
    [(real, imag)] = propagated([(exit_real, exit_imag)], tables, quarter(turn, 1.0), second=copies[6:7])
    power[...] = real * real + imag * imag
    for mode in range(power_out.shape[0]):
        outs.append(pltpu.make_async_copy(power, power_out.at[mode], sems.at[9 + mode]))
        outs[-1].start()
    wave[0] = real
    wave[1] = imag
    outs.append(pltpu.make_async_copy(wave, wave_out, sems.at[9 + power_out.shape[0]]))
    outs[-1].start()
    waited(copies[7:])
    marker = jnp.where(counts[0] > 0, cover[0], NO_TILE).astype(jnp.float32)
    own[width:, :] = jnp.full((FLAG_ROWS, width), marker)
    waited(outs)


def match(marker, tile_number):
    return (marker == tile_number).astype(jnp.float32)


def partner_kernel(own, across, combined, extra):
    width = own.shape[-1]
    core = lax.axis_index("core")
    target = (lax.axis_index(SCAN) + 1 - 2 * core).astype(jnp.float32)
    has_own = match(own[width : width + 1, :], target)
    has_across = match(across[width : width + 1, :], target)
    number = has_own + has_across
    share = 1.0 / jnp.maximum(number, 1.0)
    combined[:width, :] = (has_own * own[:width, :] + has_across * across[:width, :]) * share
    combined[width:, :] = jnp.broadcast_to(number, (FLAG_ROWS, width))
    gap = own[:width, :] - across[:width, :]
    squares = (0.5 * has_own * has_across) * (gap * gap)
    extra[...] = jnp.sum(squares.reshape(width // 8, 8, width), axis=0)


def main_kernel(
    extra, powers, own, across, beyond, partner,
    turn_in, wave_in, tables_in, tile_in, probe_in,
    chunks_out, terms,
    turn, wave, tables, tile, probe, chunks, sems,
):
    copies = fetched(
        [
            (wave_in, wave),
            (tables_in.at[pl.ds(0, 4)], tables.at[pl.ds(0, 4)]),
            (tables_in.at[pl.ds(4, 4)], tables.at[pl.ds(4, 4)]),
            (turn_in, turn),
            (tile_in, tile),
            (probe_in, probe),
        ],
        sems,
    )
    width = powers.shape[-1]
    half = width // 2
    home = lax.axis_index(SCAN).astype(jnp.float32)
    modulus = jnp.sqrt((powers[0] + powers[1]) + (powers[2] + powers[3]) + 1.0)
    mismatch_sum = jnp.zeros_like(modulus)
    squares = jnp.zeros_like(modulus)
    for ref, number in (
        (own, match(own[width : width + 1, :], home)),
        (across, match(across[width : width + 1, :], home)),
        (beyond, match(beyond[width : width + 1, :], home)),
        (partner, partner[width : width + 1, :]),
    ):
        mismatch = modulus - ref[:width, :]
        scaled = number * mismatch
        mismatch_sum += scaled
        squares += scaled * mismatch
    weight = mismatch_sum / modulus
    waited(copies[:2])
    [(real, imag)] = propagated(
        [(weight * wave[0], weight * wave[1])], tables, quarter(turn, -1.0), copies[2:3], copies[3:4]
    )
    waited(copies[4:])
    loss = jnp.full((1, half), jnp.sum(squares) + jnp.sum(extra[...]))
    blocks = width // 8
    outs = []
    for plane, value in enumerate((tile[0] * real + tile[1] * imag, tile[0] * imag - tile[1] * real)):
        for block in range(blocks):
            lines = value[8 * block : 8 * block + 8]
            start = CHUNK_ROWS * (plane * blocks + block)
            chunks[start : start + 8, :] = lines[:, :half]
            chunks[start + 8 : start + 16, :] = lines[:, half:]
            chunks[start + 16 : start + 17, :] = loss
        part = pl.ds(CHUNK_ROWS * blocks * plane, CHUNK_ROWS * blocks)
        outs.append(pltpu.make_async_copy(chunks.at[part], chunks_out.at[part], sems.at[6 + plane]))
        outs[-1].start()
    terms[0] = probe[0] * real + probe[1] * imag
    terms[1] = probe[0] * imag - probe[1] * real
    waited(outs)


def object_kernel(own_in, one_in, two_in, three_in, out, own, one, two, three, sems):
    waited(fetched([(own_in, own), (one_in, one), (two_in, two), (three_in, three)], sems))
    out[0] = (own[...] + one[...]) + (two[...] + three[...])


def plane_kernel(arrived, total):
    rows_in = arrived[...]
    count = rows_in.shape[0] // CHUNK_ROWS
    parts = [rows_in[CHUNK_ROWS * i : CHUNK_ROWS * (i + 1)] for i in range(count)]
    while len(parts) > 1:
        parts = [parts[i] + parts[i + 1] for i in range(0, len(parts), 2)]
    total[: CHUNK_ROWS] = parts[0]
    total[CHUNK_ROWS:] = jnp.zeros_like(total[CHUNK_ROWS:])


def spread_kernel(one, two, spread, loss, block, sems):
    total = one[...] + two[...]
    lines = cols(total[0:8], total[8:16])
    count = block.shape[0]
    block[...] = jnp.broadcast_to(lines[None], block.shape)
    parts = [pl.ds(i, count) for i in range(0, spread.shape[0], count)]
    copies = fetched([(block, spread.at[part]) for part in parts], sems)
    loss[...] = jnp.broadcast_to(total[16:17], loss.shape)
    waited(copies)


def struct(*shape):
    return jax.ShapeDtypeStruct(shape, jnp.float32)


def call(kernel, name, operands, outs, microseconds, copied=(), far=(), direct=(), sems=0, scratch=()):
    specs, placed = [], []
    anywhere = pl.BlockSpec(memory_space=pl.ANY)
    for index, operand in enumerate(operands):
        if operand.dtype == jnp.int32:
            specs.append(SMEM)
        else:
            specs.append(anywhere if index in copied or index in far else VMEM)
        placed.append(pltpu.with_memory_space_constraint(operand, pltpu.HBM) if index in far else operand)
    scratch_shapes = [pltpu.VMEM(operands[i].shape, operands[i].dtype) for i in copied]
    for entry in scratch:
        buffer = outs[entry] if isinstance(entry, int) else entry
        scratch_shapes.append(pltpu.VMEM(buffer.shape, buffer.dtype))
    count = len(copied) + len(direct) + sems
    if count:
        scratch_shapes.append(pltpu.SemaphoreType.DMA((count,)))
    return pl.pallas_call(
        kernel,
        out_shape=[pltpu.HBM(o.shape, o.dtype) if i in direct else o for i, o in enumerate(outs)],
        in_specs=specs,
        out_specs=[anywhere if i in direct else VMEM for i in range(len(outs))],
        scratch_shapes=scratch_shapes,
        cost_estimate=pl.CostEstimate(
            flops=int(microseconds * 1.1e9), bytes_accessed=0, transcendentals=0
        ),
        compiler_params=pltpu.CompilerParams(vmem_limit_bytes=32 * 1024 * 1024),
        name=name,
    )(*placed)


def body(scan_size, object_tiles, probe, measured, cover, counts, phase):
    width = phase.shape[-1]
    modes = lax.axis_size("mode")
    peers = lax.axis_size(PLANE)
    tables = jnp.asarray(split_tables(width))
    order = jnp.asarray(permutation(width))
    tile, own_probe = object_tiles[0], probe[0]
    square, plane_pair = struct(width, width), struct(2, width, width)
    slot = struct(width + FLAG_ROWS, width)
    own, wave, turn, power = call(
        forward_kernel, "forward", (phase, order, tile, own_probe, tables, cover, counts, measured),
        [slot, plane_pair, plane_pair, struct(modes, width, width)], 4,
        copied=(1, 2, 3, 4), far=(0, 1, 2, 3, 4, 7), direct=(1, 2, 3), sems=modes + 3,
        scratch=(struct(2, width, width // 2), 1, 2, square),
    )
    powers = lax.all_to_all(power, "mode", 0, 0, tiled=True)
    places = range(scan_size)
    edge = [(i, (i + 1) % scan_size if i % 2 else (i - 1) % scan_size) for i in places]
    across = lax.ppermute(own, SCAN, edge)
    next_chip = [(i, (i - 2) % scan_size if i % 2 else (i + 2) % scan_size) for i in places]
    beyond = lax.ppermute(own, SCAN, next_chip)
    combined, extra = call(partner_kernel, "partner", (own, across), [slot, struct(8, width)], 0)
    partner = moved(combined, "core", 1)
    chunks, terms = call(
        main_kernel, "main",
        (extra, powers, own, across, beyond, partner, turn, wave, tables, tile, own_probe),
        [struct(peers * CHUNK_ROWS, 128), plane_pair], 4,
        copied=tuple(range(6, 11)), far=(6, 7, 8, 9, 10), direct=(0,), sems=2, scratch=(0,),
    )
    arrived = lax.all_to_all(chunks.reshape(peers, 1, CHUNK_ROWS * 128), PLANE, 0, 0, tiled=True)
    others = [moved(terms, "mode", step) for step in (2, 1, 3)]
    [part] = call(plane_kernel, "plane", (arrived.reshape(peers * CHUNK_ROWS, 128),), [struct(24, 128)], 0)
    part_other = moved(part, "core", 1)
    spread, loss = call(
        spread_kernel, "spread", (part, part_other), [struct(peers, 8, width), struct(8, 128)], 0,
        direct=(0,), sems=7, scratch=(struct(peers // 8, 8, width),),
    )
    probe_total = lax.all_to_all(spread, PLANE, 0, 0, tiled=True)
    [object_total] = call(
        object_kernel, "object", (terms, *others), [struct(1, 2, width, width)], 100, copied=(0, 1, 2, 3)
    )
    return (
        object_total,
        probe_total.reshape(1, 2, width, width),
        loss[0, 0] / (scan_size * width * width),
    )


def solution(mesh):
    scan_size, modes = mesh.shape["scan"], mesh.shape["mode"]
    cube = Mesh(mesh.devices.reshape(8, 8, 2, modes), ("z", "y", "core", "mode"))
    return jax.shard_map(
        functools.partial(body, scan_size),
        mesh=cube,
        in_specs=(
            P(SCAN, None, None, None),
            P("mode", None, None, None),
            P(SCAN, None, None),
            P(SCAN),
            P(SCAN),
            P(),
        ),
        out_specs=(P(SCAN, None, None, None), P("mode", None, None, None), P()),
        check_vma=False,
    )
```
